32 devices in a mesh: row: 16 (over z, y, core), col: 2 (over x).
Axes of the slice: x: 2, y: 2, z: 4, core: 2. Of those that a mesh axis runs over, the one named last changes fastest.
Arguments:
- factor: float32 [49152, 8192], P('row', 'col'), may hold values from -0.0390625 to 0.0390625
- covariance: float32 [49152, 2048], P('row', 'col'), may hold values from -6 to 6
- inv_diagonal: float32 [8192], P(('col', 'row')), may hold values from 0.5 to 4
- columns: int32 [2048], replicated, may hold values from 0 to 8191
Outputs:
- sigma_window: float32 [8192, 2048], P(('col', 'row'))
The draws below stay inside these ranges and needn't reach their ends.
Inputs may be any that keep to these rules, and one draw needn't show every extreme that they name: `columns`: each entry is a separator index; entries may repeat.
All inputs are finite; a program needn't handle non-finite values.
Results may differ from the reference program's by a relative error of at most 0.000071.
Values sent between devices are 32-bit elements; how exact they have to be, the bound alone decides.
A program may use at most 192 MiB of HBM per device.

```python
import math
import jax
import jax.numpy as jnp
from jax import lax

S = 8192
A = 49152
W = 2048


def with_ends(array, rng, smallest, top_value):
    dims = array.shape
    index_at = [jax.random.randint(jax.random.fold_in(rng, axis), (), 0, dims[axis]) for axis in range(len(dims))]
    array = array.at[tuple(index_at)].set(smallest)
    longest = dims.index(max(dims))
    index_at[longest] = (index_at[longest] + 1) % dims[longest]
    return array.at[tuple(index_at)].set(top_value)


def with_spikes(entries, key, source, target, parts, factor):
    owner, partner = [(jnp.arange(entries.shape[position]) // (entries.shape[position] // parts)).reshape([-1 if axis == position else 1 for axis in range(entries.ndim)]) for position in (source, target)]
    chosen = jax.random.permutation(key, parts)[partner]
    strong = (owner == chosen) | (owner == (partner + parts // 2) % parts)
    return jnp.where(strong, factor * entries, entries)


def steps_of(rng, dims, split, low, largest):
    def one(position, blocks):
        heights = jax.random.uniform(jax.random.fold_in(jax.random.fold_in(rng, 6), position), (blocks,), jnp.float32, low / len(split), largest / len(split))
        return jnp.repeat(jnp.exp(heights), dims[position] // blocks).reshape((-1,) + (1,) * (len(dims) - position - 1))

    gain = one(*split[0])
    for cut in split[1:]:
        gain = gain * one(*cut)
    return gain


def gaussian(own_key, shape, scale, limit, split=(), kind=jnp.bfloat16):
    entries = scale * jax.random.normal(own_key, shape, jnp.float32)
    if split:
        entries = entries * steps_of(own_key, shape, split, -0.22, 0.18)
    return jnp.clip(entries, -limit, limit).astype(kind)


def heavy_noise(own_key, extent, deviation, reach, pieces, heavy, held_as=jnp.bfloat16):
    array = deviation * jax.random.normal(own_key, extent, jnp.float32)
    if pieces:
        array = array * steps_of(own_key, extent, pieces, -0.22, 0.18)
    return jnp.clip(with_spikes(array, jax.random.fold_in(own_key, 3), *heavy), -reach, reach).astype(held_as)


def setup_inputs(seed: int = 0) -> dict:
    arg_keys = jax.random.split(jax.random.key(seed), 5)
    return {
        "factor": heavy_noise(arg_keys[0], (A, S), A ** -0.5, 0.0390625, ((0, 16), (1, 2)), (0, 1, 16, 2.0), jnp.float32),
        "covariance": gaussian(arg_keys[1], (A, W), 1.0, 6.0, ((0, 16), (1, 2)), jnp.float32),
        "inv_diagonal": jnp.clip(jnp.exp(math.log(4.0) - 2.0794415 * jax.random.uniform(arg_keys[2], (S,), jnp.float32) ** steps_of(arg_keys[2], (S,), ((0, 32),), -0.2, 0.2)), 0.5, 4.0),
        "columns": with_ends(jax.random.randint(arg_keys[3], (W,), 0, S), jax.random.fold_in(arg_keys[3], 1), 0, S - 1).astype(jnp.int32),
    }


def reference(factor, covariance, inv_diagonal, columns):
    product = lax.dot_general(factor, covariance, (((0,), (0,)), ((), ())), precision=lax.Precision.HIGHEST, preferred_element_type=jnp.float32)
    row_ids = lax.iota(jnp.int32, inv_diagonal.shape[0])
    on_diagonal = row_ids[:, None] == columns[None, :]
    return jnp.where(on_diagonal, inv_diagonal[:, None], jnp.zeros((), jnp.float32)) - product
```

```python
import jax
import jax.numpy as jnp
from jax import lax
from jax.experimental.layout import Layout, with_layout_constraint
from jax.sharding import PartitionSpec as P


def contract_rows(left_block, right_block):
    return lax.dot_general(
        left_block,
        right_block,
        (((0,), (0,)), ((), ())),
        precision=lax.Precision.HIGH,
        preferred_element_type=jnp.float32,
    )


def widths(total, parts):
    unit = total // 8
    if unit % 128:
        return [total]
    return [unit * part for part in parts]


def per_device(factor, covariance, inv_diagonal, columns):
    row_devices, col_devices = lax.axis_size("row"), lax.axis_size("col")
    row, col = lax.axis_index("row"), lax.axis_index("col")
    width = covariance.shape[1]
    row_count = inv_diagonal.shape[0]
    core = lax.rem(row, 2)
    chips = row_devices // 2
    pairs = [(i, i ^ 1) for i in range(row_devices)]
    groups = [[2 * chip + side for chip in range(chips)] for side in range(2)]
    row_ids = (col * row_devices + row) * row_count + lax.iota(jnp.int32, row_count)

    def reduced(block, pair=()):
        partial = with_layout_constraint(contract_rows(factor, block), Layout((0, 1)))
        if pair:
            partial, *here = lax.optimization_barrier((partial, *[received[at] for at in pair]))
            for at, value in zip(pair, here):
                received[at] = value
        partial = partial.reshape(chips, 2, row_count, -1)
        give = lax.dynamic_index_in_dim(partial, 1 - core, 1, keepdims=False)
        keep = lax.dynamic_index_in_dim(partial, core, 1, keepdims=False)
        chip_sum = keep + lax.ppermute(give, "row", pairs)
        chip_sum = chip_sum.reshape(chips * row_count, -1)
        return lax.psum_scatter(
            chip_sum, "row", scatter_dimension=0, axis_index_groups=groups, tiled=True
        )

    def columns_of(start, size):
        return lax.slice_in_dim(covariance, start, start + size, axis=1)

    begins, received = [], []
    for step in range(1, col_devices):
        owner = lax.rem(col - step + col_devices, col_devices)
        shift = [(i, (i + step) % col_devices) for i in range(col_devices)]
        start = 0
        for size in widths(width, (1,) * 8):
            block = columns_of(start, size)
            if len(received) >= 2:
                block, received[-2] = lax.optimization_barrier((block, received[-2]))
            begins.append(owner * width + start)
            received.append(lax.ppermute(block, "col", shift))
            start += size

    own_parts = widths(width, (4, 4))
    owned, start = [], 0
    for size in own_parts:
        owned.append((col * width + start, columns_of(start, size)))
        start += size
    together = 2 if len(own_parts) > 1 else 1
    pairs_at = [
        list(range(first, first + together)) for first in range(0, len(received), together)
    ]

    def after(entry, pair):
        begin, block = entry
        block, *here = lax.optimization_barrier((block, *[received[at] for at in pair]))
        for at, value in zip(pair, here):
            received[at] = value
        return begin, block

    def taken(*chosen):
        return [(begins[at], received[at]) for pair in chosen for at in pair]

    waits_for = {}
    if len(own_parts) > 1 and len(pairs_at) > 3:
        plan = [[owned[0]], [after(owned[1], pairs_at[0])], taken(pairs_at[0], pairs_at[1])]
        plan += pairs_at[2:]
        waits_for = dict(enumerate(pairs_at))
    else:
        plan = [[entry] for entry in owned] + pairs_at

    out = jnp.zeros((row_count, columns.shape[0]), jnp.float32)
    for index, entries in enumerate(plan):
        if isinstance(entries[0], int):
            entries = taken(entries)
        product = reduced(
            jnp.concatenate([block for _, block in entries], axis=1),
            waits_for.get(index, ()),
        )
        start = 0
        for begin, block in entries:
            size = block.shape[1]
            ids = lax.dynamic_slice_in_dim(columns, begin, size)
            on_diagonal = row_ids[:, None] == ids[None, :]
            diagonal = jnp.where(on_diagonal, inv_diagonal[:, None], jnp.zeros((), jnp.float32))
            window = diagonal - lax.slice_in_dim(product, start, start + size, axis=1)
            out = lax.dynamic_update_slice(out, window, (0, begin))
            start += size
    return out


def solution(mesh):
    return jax.shard_map(
        per_device,
        mesh=mesh,
        in_specs=(P("row", "col"), P("row", "col"), P(("col", "row")), P()),
        out_specs=P(("col", "row"), None),
        check_vma=False,
    )
```

```python
import jax
import jax.numpy as jnp
from jax import lax
from jax.experimental.layout import Layout, with_layout_constraint
from jax.sharding import PartitionSpec as P


def contract_rows(left_block, right_block):
    return lax.dot_general(
        left_block,
        right_block,
        (((0,), (0,)), ((), ())),
        precision=lax.Precision.HIGH,
        preferred_element_type=jnp.float32,
    )


def widths(total, parts):
    unit = total // 8
    if unit % 128:
        return [total]
    return [unit * part for part in parts]


def per_device(factor, covariance, inv_diagonal, columns):
    row_devices, col_devices = lax.axis_size("row"), lax.axis_size("col")
    row, col = lax.axis_index("row"), lax.axis_index("col")
    width = covariance.shape[1]
    row_count = inv_diagonal.shape[0]
    row_ids = (col * row_devices + row) * row_count + lax.iota(jnp.int32, row_count)

    def halved(total, stride):
        side = lax.rem(row // stride, 2)
        halves = total.reshape(total.shape[0] // 2, 2, row_count, -1)
        give = lax.dynamic_index_in_dim(halves, 1 - side, 1, keepdims=False)
        keep = lax.dynamic_index_in_dim(halves, side, 1, keepdims=False)
        swap = [(i, i ^ stride) for i in range(row_devices)]
        return keep + lax.ppermute(give, "row", swap)

    def columns_of(start, size):
        return lax.slice_in_dim(covariance, start, start + size, axis=1)

    parts = widths(width, (1,) * 8)
    together = 2 if len(parts) > 1 else 1
    coming = []
    for step in range(1, col_devices):
        owner = lax.rem(col - step + col_devices, col_devices)
        shift = [(i, (i + step) % col_devices) for i in range(col_devices)]
        start = 0
        for size in parts:
            coming.append((owner * width + start, start, size, shift))
            start += size
    pairs = [coming[first : first + together] for first in range(0, len(coming), together)]
    owned, start = [], 0
    for size in widths(width, (4, 4)):
        owned.append((col * width + start, columns_of(start, size)))
        start += size

    received, sums, strides, plan = [], [], [], []

    def advance():
        for at in range(len(sums)):
            if strides[at] < row_devices:
                sums[at] = halved(sums[at], strides[at])
                strides[at] *= 2

    def multiply(entries, ready, pair):
        block = jnp.concatenate([block for _, block in entries], axis=1)
        if ready:
            block = lax.optimization_barrier((block, *ready))[0]
        partial = with_layout_constraint(contract_rows(factor, block), Layout((0, 1)))
        if pair:
            partial, *pair = lax.optimization_barrier((partial, *pair))
        plan.append([(begin, block.shape[1]) for begin, block in entries])
        sums.append(partial.reshape(row_devices, row_count, -1))
        strides.append(1)
        return pair

    waiting = owned
    for index, pair in enumerate(pairs):
        ready = [total for total, stride in zip(sums, strides) if 1 < stride < row_devices]
        advance()
        blocks = [columns_of(start, size) for _, start, size, _ in pair]
        if received:
            ready = ready + received
        if ready:
            blocks = lax.optimization_barrier((*blocks, *ready))[: len(blocks)]
        arriving = [lax.ppermute(block, "col", entry[3]) for block, entry in zip(blocks, pair)]
        if index == 1 and len(waiting) == 1:
            begin, block = waiting[0]
            waiting = [(begin, lax.optimization_barrier((block, *received))[0])]
        if index < len(owned):
            taken, waiting = waiting[:1], waiting[1:]
        else:
            taken, waiting = waiting, []
        arriving = multiply(taken, [], arriving)
        waiting = waiting + [(entry[0], block) for entry, block in zip(pair, arriving)]
        received = arriving
    ready = [total for total, stride in zip(sums, strides) if 1 < stride < 8]
    sums[-1], strides[-1] = halved(sums[-1], 1), 2
    ready.append(sums[-1])
    advance()
    beside = [at for at in range(len(sums)) if strides[at] == 4]
    for at, total in zip(beside, multiply(waiting, ready, [sums[at] for at in beside])):
        sums[at] = total
    while min(strides) < row_devices:
        advance()

    out = jnp.zeros((row_count, columns.shape[0]), jnp.float32)
    for entries, total in zip(plan, sums):
        product = total.reshape(row_count, -1)
        start = 0
        for begin, size in entries:
            ids = lax.dynamic_slice_in_dim(columns, begin, size)
            on_diagonal = row_ids[:, None] == ids[None, :]
            diagonal = jnp.where(on_diagonal, inv_diagonal[:, None], jnp.zeros((), jnp.float32))
            window = diagonal - lax.slice_in_dim(product, start, start + size, axis=1)
            out = lax.dynamic_update_slice(out, window, (0, begin))
            start += size
    return out


def solution(mesh):
    return jax.shard_map(
        per_device,
        mesh=mesh,
        in_specs=(P("row", "col"), P("row", "col"), P(("col", "row")), P()),
        out_specs=P(("col", "row"), None),
        check_vma=False,
    )
```
